128 devices in a mesh: prompt: 4 (over z_lo, core), seq: 32 (over y, x, z_hi).
Axes of the slice: x: 4, y: 4, z: 4 (z_hi: 2, z_lo: 2; z = z_hi * 2 + z_lo), core: 2. Of those that a mesh axis runs over, the one named last changes fastest.
Arguments:
- resp_q: bfloat16 [32768, 8192], P(('prompt', 'seq')), may hold values from -8 to 8
- resp_k: bfloat16 [32768, 1024], P(('prompt', 'seq')), may hold values from -6 to 6
- resp_v: bfloat16 [32768, 1024], P(('prompt', 'seq')), may hold values from -6 to 6
- prefix_k: bfloat16 [4096, 1024], P(('prompt', 'seq')), may hold values from -6 to 6
- prefix_v: bfloat16 [4096, 1024], P(('prompt', 'seq')), may hold values from -6 to 6
- destination: int32 [32768], replicated, may hold values from 0 to 32767, as said below
- resp_len: int32 [4, 16], P('prompt'), may hold values from 1 to 768, 8192 in all within a row
Outputs:
- attended: bfloat16 [32768, 8192], P(('prompt', 'seq'))
The draws below stay inside these ranges and needn't reach their ends.
Inputs may be any that keep to these rules, and one draw needn't show every extreme that they name: `destination`: A permutation of the 32768 positions; device i of the mesh (prompt index times 32 plus seq index) holds rollout rows i * 256 onwards and owns positions i * 256 onwards. From one device to one device go either exactly 2 rows or none.
All inputs are finite; a program needn't handle non-finite values.
Results may differ from the reference program's by a relative error of at most 0.0059.
Values may be sent and summed in bfloat16 or wider, within the bound.
A program may use at most 256 MiB of HBM per device.

```python
import math
import jax
import jax.numpy as jnp
import numpy as np
from jax import lax

H = 64
KVH = 8
HD = 128
R_DEV = 256
PRE_DEV = 32
RESP = 16
MOST = 768
PREFIX = 1024
ROWS_ALL = 32768
CAP = 2
N_PROMPT = 4
N_SEQ = 32
DEVICES = 128


def draw_resp_q(key, part):
    key = jax.random.fold_in(key, 1)
    total_rows = DEVICES * R_DEV
    result = jnp.clip(2.5 * jax.random.normal(key, (total_rows, H * HD), jnp.float32), -8.0, 8.0)
    return result.astype(jnp.bfloat16)


def draw_prefix_k(key, part):
    key = jax.random.fold_in(key, 3)
    total_rows = N_PROMPT * PREFIX
    result = jnp.clip(jax.random.normal(key, (total_rows, KVH * HD), jnp.float32), -6.0, 6.0)
    return result.astype(jnp.bfloat16)


def draw_destination(key, part):
    key = jax.random.fold_in(key, 2)
    key_one, key_two, key_three, key_four = jax.random.split(key, 4)
    n_devices = DEVICES
    n_rows = R_DEV
    offsets = jax.random.permutation(key_one, n_devices)[:n_rows // CAP]
    repeated = jnp.repeat(offsets, CAP)
    orders = jax.vmap(lambda single: jax.random.permutation(single, n_rows))(jax.random.split(key_two, n_devices))
    chosen = repeated[orders]
    relabel = jax.random.permutation(key_three, n_devices)
    sources = jnp.arange(n_devices)[:, None]
    targets = relabel[(chosen + sources) % n_devices].reshape(-1)
    shuffled = jax.random.permutation(key_four, n_devices * n_rows)
    sorted_ids = shuffled[jnp.argsort(targets[shuffled], stable=True)]
    placed = jnp.zeros((n_devices * n_rows,), jnp.int32).at[sorted_ids].set(jnp.arange(n_devices * n_rows, dtype=jnp.int32))
    return placed


def block_levels(own_key, shape, pieces, low, largest):
    loudness = 1.0
    for dim, blocks in pieces:
        draws = jax.random.uniform(jax.random.fold_in(jax.random.fold_in(own_key, 6), dim), (blocks,), jnp.float32, low / len(pieces), largest / len(pieces))
        loudness = loudness * jnp.repeat(jnp.exp(draws), shape[dim] // blocks).reshape((-1,) + (1,) * (len(shape) - 1 - dim))
    return loudness


def length_profile(count, total, most, skew):
    weights = [(1 << 20) // math.isqrt(grade ** skew) + 1 for grade in range(2, count + 1)]
    surplus, holding = total - most - (count - 1), [1] * (count - 1)
    while surplus > 0:
        candidates = [i for i in range(count - 1) if holding[i] < most]
        whole, remaining = sum([weights[i] for i in candidates]), surplus
        for i in candidates:
            more = min(most - holding[i], max(1, remaining * weights[i] // whole), surplus)
            holding[i] = holding[i] + more
            surplus = surplus - more
    return np.array([most] + holding)


def uneven(own_key, amount, total, limit, skew):
    if amount == 2:
        one = jax.random.randint(own_key, (), max(1, total - limit), min(limit, total - 1) + 1)
        return jnp.stack([one, total - one])
    sizes = jnp.asarray(length_profile(amount, total, limit, skew), jnp.int32)
    twos = (amount - 1) // 2
    donor, receiver = sizes[1:1 + 2 * twos:2], sizes[2:2 + 2 * twos:2]
    room = jnp.minimum(donor - 1, limit - receiver)
    moved = jax.random.randint(jax.random.fold_in(own_key, 1), (twos,), 0, 1 << 20) % (room + 1)
    sizes = sizes.at[1:1 + 2 * twos:2].set(donor - moved).at[2:2 + 2 * twos:2].set(receiver + moved)
    return sizes[jax.random.permutation(jax.random.fold_in(own_key, 2), amount)]


def noise(stream_key, shape, width, bound, shards=(), kind=jnp.bfloat16):
    level = block_levels(stream_key, shape, shards, -0.22, 0.18) if shards else 1.0
    values = jax.random.normal(stream_key, shape, jnp.float32) * width * level
    return jnp.minimum(jnp.maximum(values, -bound), bound).astype(kind)


def setup_inputs(seed: int = 0) -> dict:
    keys = jax.random.split(jax.random.key(seed), 8)
    return {
        "resp_q": draw_resp_q(jax.random.fold_in(keys[7], 71), 0),
        "resp_k": noise(keys[1], (ROWS_ALL, KVH * HD), 1.0, 6.0, ((0, 128),)),
        "resp_v": noise(keys[2], (ROWS_ALL, KVH * HD), 1.0, 6.0, ((0, 128),)),
        "prefix_k": draw_prefix_k(jax.random.fold_in(keys[7], 71), 0),
        "prefix_v": noise(keys[4], (N_PROMPT * PREFIX, KVH * HD), 1.0, 6.0, ((0, 128),)),
        "destination": draw_destination(jax.random.fold_in(keys[7], 71), 0),
        "resp_len": jax.vmap(lambda own: uneven(own, RESP, N_SEQ * R_DEV, MOST, 2))(jax.random.split(keys[6], N_PROMPT)).reshape((N_PROMPT, RESP)).astype(jnp.int32),
    }


def block_attend(queries, pre_keys, pre_values, near_keys, near_values, allowed, scaling):
    queries32 = queries.astype(jnp.float32)
    far_scores = jnp.einsum('rkgd,nkd->rkgn', queries32, pre_keys.astype(jnp.float32)) * scaling
    near_scores = jnp.einsum('rkgd,nkd->rkgn', queries32, near_keys.astype(jnp.float32)) * scaling
    near_scores = jnp.where(allowed[:, None, None, :], near_scores, -jnp.inf)
    scores = jnp.concatenate([far_scores, near_scores], axis=-1)
    top_score = lax.optimization_barrier(jnp.max(scores, axis=-1, keepdims=True))
    weights = jnp.exp(scores - top_score)
    totals = lax.optimization_barrier(jnp.sum(weights, axis=-1))
    rounded = lax.optimization_barrier(weights.astype(jnp.bfloat16)).astype(jnp.float32)
    values32 = jnp.concatenate([pre_values, near_values], axis=0).astype(jnp.float32)
    mixed = jnp.einsum('rkgn,nkd->rkgd', rounded, values32) / totals[..., None]
    return mixed.astype(jnp.bfloat16)

def reference(resp_q, resp_k, resp_v, prefix_k, prefix_v, destination, resp_len):
    total_rows = resp_q.shape[0]
    source_of = jnp.zeros((total_rows,), jnp.int32).at[destination].set(jnp.arange(total_rows, dtype=jnp.int32))
    queries = resp_q[source_of]
    keys_all = resp_k[source_of]
    values_all = resp_v[source_of]
    group_rows = N_SEQ * R_DEV
    prefix_len = PRE_DEV * N_SEQ
    per_kv = H // KVH
    block = math.gcd(group_rows, 512)
    margin = -(-MOST // block) * block
    scaling = 1.0 / math.sqrt(HD)
    outputs = []
    for prompt in range(N_PROMPT):
        low = prompt * group_rows
        q_group = queries[low:low + group_rows].reshape(group_rows, KVH, per_kv, HD)
        k_group = keys_all[low:low + group_rows].reshape(group_rows, KVH, HD)
        v_group = values_all[low:low + group_rows].reshape(group_rows, KVH, HD)
        pre_low = prompt * prefix_len
        pre_keys = prefix_k[pre_low:pre_low + prefix_len].reshape(prefix_len, KVH, HD)
        pre_values = prefix_v[pre_low:pre_low + prefix_len].reshape(prefix_len, KVH, HD)
        lengths = resp_len[prompt]
        finish = jnp.cumsum(lengths)
        row_ids = jnp.arange(group_rows, dtype=jnp.int32)
        starts = lax.optimization_barrier(jnp.sum(jnp.where(finish[None, :] <= row_ids[:, None], lengths[None, :], 0), axis=1)).astype(jnp.int32)
        padded_k = jnp.concatenate([jnp.zeros((margin, KVH, HD), k_group.dtype), k_group], axis=0)
        padded_v = jnp.concatenate([jnp.zeros((margin, KVH, HD), v_group.dtype), v_group], axis=0)

        def one_block(index, q_group=q_group, padded_k=padded_k, padded_v=padded_v, starts=starts, pre_keys=pre_keys, pre_values=pre_values):
            first = (index * block).astype(jnp.int32)
            q_block = lax.dynamic_slice_in_dim(q_group, first, block)
            near_keys = lax.dynamic_slice_in_dim(padded_k, first, margin + block)
            near_values = lax.dynamic_slice_in_dim(padded_v, first, margin + block)
            key_ids = first - margin + jnp.arange(margin + block, dtype=jnp.int32)
            query_ids = first + jnp.arange(block, dtype=jnp.int32)
            start_block = lax.dynamic_slice_in_dim(starts, first, block)
            allowed = (key_ids[None, :] >= start_block[:, None]) & (key_ids[None, :] <= query_ids[:, None])
            return block_attend(q_block, pre_keys, pre_values, near_keys, near_values, allowed, scaling)
        results = lax.map(one_block, jnp.arange(group_rows // block, dtype=jnp.int32))
        outputs.append(results.reshape(group_rows, H * HD))
    return jnp.concatenate(outputs, axis=0)
```

```python
import functools
import math

import jax
import jax.numpy as jnp
from jax import lax
from jax.experimental import pallas as pl
from jax.experimental.pallas import tpu as pltpu
from jax.sharding import PartitionSpec as P

MESH = pl.DeviceIdType.MESH
N = 128
NS = 32
ROWS = 256
GROUPS = 8
PER = 8
HD = 128
NEAR = 1024
PRE = 1024
KEYS = PRE + NEAR
WIDE = 512
SCALE = math.log2(math.e) / math.sqrt(HD)
BF = jnp.bfloat16
F32 = jnp.float32


def device_of(index):
    return (index // NS, lax.rem(index, NS))


def remote(src, dst, send, recv, device):
    return pltpu.make_async_remote_copy(
        src_ref=src, dst_ref=dst, send_sem=send, recv_sem=recv, device_id=device, device_id_type=MESH
    )


def await_bytes(ref, sem):
    pltpu.make_async_copy(ref, ref, sem).wait()


def iota(shape, dim):
    return lax.broadcasted_iota(jnp.int32, shape, dim).astype(F32)


def kernel(
    q_ref, k_ref, v_ref, pk_ref, pv_ref, dest_ref, dest_t_ref, len_ref, out_ref,
    send_q, send_kv, got_q, got_kv, pre_k, pre_v, stage_q, stage_kv, near,
    lhs, keys2, vals2, mask, back, scores, heads_out,
    q_send, q_recv, kv_send, kv_recv, pre_send, pre_recv,
):
    mp = lax.axis_index("prompt")
    ms = lax.axis_index("seq")
    me = mp * NS + ms
    my, mx, mz = ms // 8, lax.rem(ms // 2, 4), lax.rem(ms, 2)

    barrier = pltpu.get_barrier_semaphore()

    def greet(i, carry):
        pl.semaphore_signal(
            barrier, inc=1, device_id=device_of(lax.rem(me + i, N)), device_id_type=MESH
        )
        return carry

    lax.fori_loop(1, N, greet, 0)

    dest_t = dest_t_ref[...].astype(F32)
    own_row = dest_ref[pl.ds(me, 1), :].astype(F32)
    me_f = me.astype(F32)
    own_col = jnp.sum(jnp.where(iota((ROWS, N), 1) == me_f, dest_t, 0.0), axis=1, keepdims=True)
    slot = jnp.sum((own_col < own_row).astype(F32), axis=0, keepdims=True)
    packer = (iota((ROWS, ROWS), 0) == slot).astype(BF)

    send_kv[pl.ds(0, 96), :] = jnp.zeros((96, HD), BF)
    for half, ref in enumerate((k_ref, v_ref)):
        packed = jnp.dot(packer, ref[...], preferred_element_type=F32)
        for g in range(GROUPS):
            stage_kv[pl.ds(half * GROUPS + g, ROWS, stride=16), :] = packed[:, g * HD:(g + 1) * HD]
    send_kv[pl.ds(96, 4096), :] = stage_kv[...].astype(BF)
    pre_k[my, mx, mz] = pk_ref[...]
    pre_v[my, mx, mz] = pv_ref[...]
    got_kv[pl.ds(pl.multiple_of(me * 128, 128), 128), :] = send_kv[
        pl.ds(pl.multiple_of(me * 32, 32), 128), :
    ]

    def pack(g, carry):
        packed = jnp.dot(
            packer, q_ref[:, pl.ds(pl.multiple_of(g * 1024, 1024), 1024)],
            preferred_element_type=F32,
        )
        for j in range(PER):
            stage_q[pl.ds(j, ROWS, stride=PER), :] = packed[:, j * HD:(j + 1) * HD]
        send_q[g] = stage_q[...].astype(BF)
        own = pl.ds(pl.multiple_of(me * 16, 16), 16)
        got_q[g, own, :] = send_q[g, own, :]
        return carry

    lax.fori_loop(0, GROUPS, pack, 0)

    pl.semaphore_wait(barrier, N - 1)

    def along_x(k):
        return (mp, my * 8 + lax.rem(mx + k, 4) * 2 + mz)

    def along_y(k):
        return (mp, lax.rem(my + k, 4) * 8 + mx * 2 + mz)

    across = (mp, ms + 1 - 2 * mz)
    for i, ref in enumerate((pre_k, pre_v)):
        own = ref.at[my, mx, mz]
        remote(own, own, pre_send.at[i], pre_recv.at[i], across).start()

    def spread_kv(i, carry):
        to = lax.rem(me + i, N)
        remote(
            send_kv.at[pl.ds(pl.multiple_of(to * 32, 32), 128)],
            got_kv.at[pl.ds(pl.multiple_of(me * 128, 128), 128)],
            kv_send, kv_recv, device_of(to),
        ).start()
        return carry

    lax.fori_loop(1, N, spread_kv, 0)

    for i, ref in enumerate((pre_k, pre_v)):
        await_bytes(ref.at[0, 0, 0], pre_recv.at[i])
    for k in (1, 3, 2):
        remote(pre_k.at[my, mx], pre_k.at[my, mx], pre_send.at[2], pre_recv.at[2], along_x(k)).start()
        remote(pre_v.at[my, mx], pre_v.at[my, mx], pre_send.at[3], pre_recv.at[3], along_y(k)).start()

    def spread_q(n, carry):
        g, i = n // (N - 1), lax.rem(n, N - 1) + 1
        to = lax.rem(me + i, N)
        remote(
            send_q.at[g, pl.ds(pl.multiple_of(to * 16, 16), 16)],
            got_q.at[g, pl.ds(pl.multiple_of(me * 16, 16), 16)],
            q_send.at[g], q_recv.at[g], device_of(to),
        ).start()
        return carry

    lax.fori_loop(0, 2 * (N - 1), spread_q, 0)
    await_bytes(pre_k.at[0, pl.ds(0, 3)], pre_recv.at[2])
    await_bytes(pre_v.at[pl.ds(0, 3), 0], pre_recv.at[3])
    for k in (1, 3, 2):
        remote(pre_k.at[my], pre_k.at[my], pre_send.at[4], pre_recv.at[4], along_y(k)).start()
        remote(pre_v.at[:, mx], pre_v.at[:, mx], pre_send.at[5], pre_recv.at[5], along_x(k)).start()
    lax.fori_loop(2 * (N - 1), GROUPS * (N - 1), spread_q, 0)

    dest = dest_ref[...].astype(F32)
    base = me_f * ROWS
    here = (dest >= base) & (dest < base + ROWS)
    pos_q = jnp.concatenate(
        [
            jnp.min(jnp.where(here, dest, 1e9), axis=1, keepdims=True),
            jnp.max(jnp.where(here, dest, -1.0), axis=1, keepdims=True),
        ],
        axis=0,
    )
    prompt_base = (mp * (NS * ROWS)).astype(F32)
    start = jnp.zeros((ROWS, 1), F32) + prompt_base
    finish = prompt_base
    for c in range(16):
        length = len_ref[0, c].astype(F32)
        finish = finish + length
        start = start + jnp.where(pos_q >= finish, length, 0.0)
    pos_rows = []
    for k in range(4):
        low = base + (k - 3) * ROWS
        inside = (dest_t >= low) & (dest_t < low + ROWS)
        first = jnp.min(jnp.where(inside, dest_t, 1e9), axis=0, keepdims=True)
        last = jnp.max(jnp.where(inside, dest_t, -1.0), axis=0, keepdims=True)
        pos_rows.append((first, last))
    for k in range(4):
        for r in range(2):
            pos_k = pos_rows[k][r]
            mask[:, (2 * k + r) * N:(2 * k + r + 1) * N] = jnp.where(
                (pos_k >= start) & (pos_k <= pos_q), 0.0, -1e30
            )
    for r in range(2):
        back[:, r * N:(r + 1) * N] = (iota((ROWS, N), 0) == pos_rows[3][r] - base).astype(BF)
    vals2[:, HD:] = jnp.ones((KEYS, HD), BF)

    await_bytes(got_kv.at[pl.ds(0, (N - 1) * 128)], kv_recv)

    def unpack_kv(p, carry):
        stage_kv[...] = got_kv[pl.ds(pl.multiple_of(p * 4096, 4096), 4096), :].astype(F32)
        for x in range(16):
            for kr in range(8):
                near[x, pl.ds(pl.multiple_of(kr * N + p * 32, 32), 32), :] = stage_kv[
                    pl.ds(kr * 16 + x, 32, stride=128), :
                ].astype(BF)
        return carry

    lax.fori_loop(0, 4, unpack_kv, 0)
    await_bytes(pre_k.at[pl.ds(0, 3)], pre_recv.at[4])
    await_bytes(pre_v.at[:, pl.ds(0, 3)], pre_recv.at[5])

    def attend(g, carry):
        columns = pl.ds(pl.multiple_of(g * HD, HD), HD)
        for y in range(4):
            prefix_keys = pre_k[y, :, :, :, columns].reshape(256, HD)
            rows = pl.ds(y * 256, 256)
            keys2[rows, :HD] = prefix_keys
            keys2[rows, HD:] = prefix_keys
            vals2[rows, :HD] = pre_v[y, :, :, :, columns].reshape(256, HD)
        keys2[PRE:, :HD] = near[g]
        keys2[PRE:, HD:] = near[g]
        vals2[PRE:, :HD] = near[GROUPS + g]
        await_bytes(got_q.at[g, pl.ds(0, (N - 1) * 16)], q_recv.at[g])
        stage_q[...] = got_q[g].astype(F32)
        for j in range(PER):
            for r in range(2):
                scaled = stage_q[pl.ds(r * PER + j, N, stride=16), :] * SCALE
                high = scaled.astype(BF)
                lhs[j, r * N:(r + 1) * N, :HD] = high
                lhs[j, r * N:(r + 1) * N, HD:] = (scaled - high.astype(F32)).astype(BF)

        def head(j, inner):
            queries = lhs[j]
            top = None
            for c in range(KEYS // WIDE):
                part = lax.dot_general(
                    queries, keys2[c * WIDE:(c + 1) * WIDE, :], (((1,), (1,)), ((), ())),
                    preferred_element_type=F32,
                )
                if c * WIDE >= PRE:
                    part = part + mask[:, c * WIDE - PRE:(c + 1) * WIDE - PRE]
                scores[:, c * WIDE:(c + 1) * WIDE] = part
                for t in range(WIDE // HD):
                    tile = part[:, t * HD:(t + 1) * HD]
                    top = tile if top is None else jnp.maximum(top, tile)
            top = jnp.max(top, axis=1, keepdims=True)
            total = jnp.zeros((ROWS, 2 * HD), F32)
            for c in range(KEYS // WIDE):
                weights = jnp.exp2(scores[:, c * WIDE:(c + 1) * WIDE] - top).astype(BF)
                total = total + jnp.dot(
                    weights, vals2[c * WIDE:(c + 1) * WIDE, :], preferred_element_type=F32
                )
            heads_out[:, pl.ds(pl.multiple_of(j * HD, HD), HD)] = (
                total[:, :HD] / total[:, HD:]
            ).astype(BF)
            return inner

        lax.fori_loop(0, PER, head, 0)
        out_ref[:, pl.ds(pl.multiple_of(g * 1024, 1024), 1024)] = jnp.dot(
            back[...], heads_out[...], preferred_element_type=F32
        ).astype(BF)
        return carry

    lax.fori_loop(0, GROUPS, attend, 0)

    def sent_q(g, carry):
        await_bytes(send_q.at[g, pl.ds(0, (N - 1) * 16)], q_send.at[g])
        return carry

    lax.fori_loop(0, GROUPS, sent_q, 0)
    await_bytes(got_kv.at[pl.ds(0, (N - 1) * 128)], kv_send)
    for i, ref in enumerate((pre_k, pre_v)):
        await_bytes(ref.at[0, 0, 0], pre_send.at[i])
    await_bytes(pre_k.at[0, pl.ds(0, 3)], pre_send.at[2])
    await_bytes(pre_v.at[pl.ds(0, 3), 0], pre_send.at[3])
    await_bytes(pre_k.at[pl.ds(0, 3)], pre_send.at[4])
    await_bytes(pre_v.at[:, pl.ds(0, 3)], pre_send.at[5])


def per_device(resp_q, resp_k, resp_v, prefix_k, prefix_v, destination, resp_len):
    dest = destination.reshape(N, ROWS)
    vmem = pl.BlockSpec(memory_space=pltpu.VMEM)
    return pl.pallas_call(
        kernel,
        out_shape=jax.ShapeDtypeStruct((ROWS, GROUPS * PER * HD), BF),
        in_specs=[vmem] * 7 + [pl.BlockSpec(memory_space=pltpu.SMEM)],
        out_specs=vmem,
        scratch_shapes=[
            pltpu.VMEM((GROUPS, N * 16, HD), BF),
            pltpu.VMEM((131 * 32, HD), BF),
            pltpu.VMEM((GROUPS, N * 16, HD), BF),
            pltpu.VMEM((N * 128, HD), BF),
            pltpu.VMEM((4, 4, 2, 32, 1024), BF),
            pltpu.VMEM((4, 4, 2, 32, 1024), BF),
            pltpu.VMEM((N * 16, HD), F32),
            pltpu.VMEM((N * 32, HD), F32),
            pltpu.VMEM((16, NEAR, HD), BF),
            pltpu.VMEM((PER, ROWS, 2 * HD), BF),
            pltpu.VMEM((KEYS, 2 * HD), BF),
            pltpu.VMEM((KEYS, 2 * HD), BF),
            pltpu.VMEM((ROWS, NEAR), F32),
            pltpu.VMEM((ROWS, ROWS), BF),
            pltpu.VMEM((ROWS, KEYS), F32),
            pltpu.VMEM((ROWS, PER * HD), BF),
            pltpu.SemaphoreType.DMA((GROUPS,)),
            pltpu.SemaphoreType.DMA((GROUPS,)),
            pltpu.SemaphoreType.DMA,
            pltpu.SemaphoreType.DMA,
            pltpu.SemaphoreType.DMA((6,)),
            pltpu.SemaphoreType.DMA((6,)),
        ],
        compiler_params=pltpu.CompilerParams(
            collective_id=0, has_side_effects=True, vmem_limit_bytes=60 * 1024 * 1024
        ),
    )(resp_q, resp_k, resp_v, prefix_k, prefix_v, dest, dest.T, resp_len)


def solution(mesh):
    both = P(("prompt", "seq"), None)
    return jax.shard_map(
        per_device,
        mesh=mesh,
        in_specs=(both, both, both, both, both, P(), P("prompt", None)),
        out_specs=both,
        check_vma=False,
    )
```

```python
import functools
import math

import jax
import jax.numpy as jnp
from jax import lax
from jax.experimental import pallas as pl
from jax.experimental.pallas import tpu as pltpu
from jax.sharding import PartitionSpec as P

MESH = pl.DeviceIdType.MESH
N = 128
NS = 32
ROWS = 256
GROUPS = 8
PER = 8
HD = 128
NEAR = 1024
PRE = 1024
KEYS = PRE + NEAR
WIDE = 256
TILE = 512
TILES = PER * ROWS // TILE
SCALE = math.log2(math.e) / math.sqrt(HD)
HALF = 4
LATE = 8
BF = jnp.bfloat16
F32 = jnp.float32


def device_of(index):
    return (index >> 5, index & (NS - 1))


def remote(src, dst, send, recv, device):
    return pltpu.make_async_remote_copy(
        src_ref=src, dst_ref=dst, send_sem=send, recv_sem=recv, device_id=device, device_id_type=MESH
    )


def await_bytes(ref, sem):
    pltpu.make_async_copy(ref, ref, sem).wait()


def iota(shape, dim):
    return lax.broadcasted_iota(jnp.int32, shape, dim).astype(F32)


def kernel(
    q_ref, k_ref, v_ref, pk_ref, pv_ref, dest_ref, dest_t_ref, len_ref, out_ref,
    send_q, send_kv, got_q, got_kv, pre_k, pre_v, stage_q, stage_kv, near,
    lhs, keys2, vals2, mask, back, scores_a, scores_b, peak_a, peak_b, heads_out,
    q_send, q_recv, kv_send, kv_recv, pre_send, pre_recv,
):
    mp = lax.axis_index("prompt")
    ms = lax.axis_index("seq")
    me = mp * NS + ms
    my, mx, mz = ms // 8, lax.rem(ms // 2, 4), lax.rem(ms, 2)

    barrier = pltpu.get_barrier_semaphore()

    def greet(i, carry):
        pl.semaphore_signal(
            barrier, inc=1, device_id=device_of((me + i) & (N - 1)), device_id_type=MESH
        )
        return carry

    lax.fori_loop(1, N, greet, 0)

    dest_t = dest_t_ref[...].astype(F32)
    own_row = dest_ref[pl.ds(me, 1), :].astype(F32)
    me_f = me.astype(F32)
    own_col = jnp.sum(jnp.where(iota((ROWS, N), 1) == me_f, dest_t, 0.0), axis=1, keepdims=True)
    slot = jnp.sum((own_col < own_row).astype(F32), axis=0, keepdims=True)
    packer = (iota((ROWS, ROWS), 0) == slot).astype(BF)

    for i, ref in enumerate((k_ref, v_ref)):
        packed = jnp.dot(packer, ref[...], preferred_element_type=F32)
        for g in range(GROUPS):
            stage_kv[g // HALF, pl.ds(i * HALF + g % HALF, ROWS, stride=8), :] = packed[
                :, g * HD:(g + 1) * HD
            ]
    for h in range(2):
        send_kv[h, pl.ds(0, 48), :] = jnp.zeros((48, HD), BF)
        send_kv[h, pl.ds(48, 2048), :] = stage_kv[h].astype(BF)
        got_kv[h, pl.ds(pl.multiple_of(me * 64, 64), 64), :] = send_kv[
            h, pl.ds(pl.multiple_of(me * 16, 16), 64), :
        ]
        pre_k[h, my, mx, mz] = pk_ref[:, h * HALF * HD:(h + 1) * HALF * HD]
        pre_v[h, my, mx, mz] = pv_ref[:, h * HALF * HD:(h + 1) * HALF * HD]

    pl.semaphore_wait(barrier, N - 1)

    def along_x(k):
        return (mp, my * 8 + lax.rem(mx + k, 4) * 2 + mz)

    def along_y(k):
        return (mp, lax.rem(my + k, 4) * 8 + mx * 2 + mz)

    across = (mp, ms + 1 - 2 * mz)
    for i, ref in enumerate((pre_k, pre_v)):
        own = ref.at[:, my, mx, mz]
        remote(own, own, pre_send.at[i], pre_recv.at[i], across).start()

    def spread_kv(h, i):
        to = (me + i) & (N - 1)
        remote(
            send_kv.at[h, pl.ds(pl.multiple_of(to * 16, 16), 64)],
            got_kv.at[h, pl.ds(pl.multiple_of(me * 64, 64), 64)],
            kv_send.at[h], kv_recv.at[h], device_of(to),
        ).start()

    def spread_kv_part(h, first, last):
        def one(i, carry):
            spread_kv(h, i)
            return carry

        lax.fori_loop(first, last, one, 0, unroll=4)

    def spread_prefix(h, first):
        def one(n, carry):
            k, b = (n >> 2) + 1, n & 3
            piece = pre_k.at[h, my, b]
            remote(piece, piece, pre_send.at[4 + 2 * h], pre_recv.at[4 + 2 * h], along_y(k)).start()
            spread_kv(h, first + 2 * n)
            piece = pre_v.at[h, b, mx]
            remote(piece, piece, pre_send.at[5 + 2 * h], pre_recv.at[5 + 2 * h], along_x(k)).start()
            spread_kv(h, first + 2 * n + 1)
            return carry

        lax.fori_loop(0, 12, one, 0)

    spread_kv_part(0, 1, 41)
    for i, ref in enumerate((pre_k, pre_v)):
        await_bytes(ref.at[:, 0, 0, 0], pre_recv.at[i])
    for k in (1, 3, 2):
        piece = pre_k.at[:, my, mx]
        remote(piece, piece, pre_send.at[2], pre_recv.at[2], along_x(k)).start()
        piece = pre_v.at[:, my, mx]
        remote(piece, piece, pre_send.at[3], pre_recv.at[3], along_y(k)).start()
    spread_kv_part(0, 41, 81)

    def pack(g, carry):
        packed = jnp.dot(
            packer, q_ref[:, pl.ds(pl.multiple_of(g * 1024, 1024), 1024)],
            preferred_element_type=F32,
        )
        for j in range(PER):
            stage_q[pl.ds(j, ROWS, stride=PER), :] = packed[:, j * HD:(j + 1) * HD]
        send_q[g] = stage_q[...].astype(BF)
        own = pl.ds(pl.multiple_of(me * 16, 16), 16)
        got_q[g, own, :] = send_q[g, own, :]
        return carry

    lax.fori_loop(0, GROUPS, pack, 0)

    dest = dest_ref[...].astype(F32)
    base = me_f * ROWS
    here = (dest >= base) & (dest < base + ROWS)
    pos_q = jnp.concatenate(
        [
            jnp.min(jnp.where(here, dest, 1e9), axis=1, keepdims=True),
            jnp.max(jnp.where(here, dest, -1.0), axis=1, keepdims=True),
        ],
        axis=0,
    )
    prompt_base = (mp * (NS * ROWS)).astype(F32)
    start = jnp.zeros((ROWS, 1), F32) + prompt_base
    finish = prompt_base
    for c in range(16):
        length = len_ref[0, c].astype(F32)
        finish = finish + length
        start = start + jnp.where(pos_q >= finish, length, 0.0)
    pos_rows = []
    for k in range(4):
        low = base + (k - 3) * ROWS
        inside = (dest_t >= low) & (dest_t < low + ROWS)
        first = jnp.min(jnp.where(inside, dest_t, 1e9), axis=0, keepdims=True)
        last = jnp.max(jnp.where(inside, dest_t, -1.0), axis=0, keepdims=True)
        pos_rows.append((first, last))
    for k in range(4):
        for r in range(2):
            pos_k = pos_rows[k][r]
            mask[:, (2 * k + r) * N:(2 * k + r + 1) * N] = jnp.where(
                (pos_k >= start) & (pos_k <= pos_q), 0.0, -1e30
            )
    for r in range(2):
        back[:, r * N:(r + 1) * N] = (iota((ROWS, N), 0) == pos_rows[3][r] - base).astype(BF)
    vals2[:, HD:] = jnp.ones((KEYS, HD), BF)

    def spread_q(g, carry):
        def one(i, inner):
            to = (me + i) & (N - 1)
            remote(
                send_q.at[g, pl.ds(pl.multiple_of(to * 16, 16), 16)],
                got_q.at[g, pl.ds(pl.multiple_of(me * 16, 16), 16)],
                q_send.at[g], q_recv.at[g], device_of(to),
            ).start()
            return inner

        return lax.fori_loop(1, N, one, carry, unroll=8)

    await_bytes(pre_k.at[:, 0, pl.ds(0, 3)], pre_recv.at[2])
    await_bytes(pre_v.at[:, pl.ds(0, 3), 0], pre_recv.at[3])
    spread_prefix(0, 81)
    spread_kv_part(0, 105, N)
    lax.fori_loop(0, HALF, spread_q, 0)
    spread_kv_part(1, 1, 41)
    spread_prefix(1, 41)
    spread_kv_part(1, 65, N)
    lax.fori_loop(HALF, LATE, spread_q, 0)

    def unpack_kv(h):
        def one(p, carry):
            stage_kv[0] = got_kv[h, pl.ds(pl.multiple_of(p * 2048, 2048), 2048), :].astype(F32)
            for x in range(8):
                for kr in range(8):
                    near[x // HALF, h * HALF + x % HALF, pl.ds(pl.multiple_of(kr * N + p * 32, 32), 32), :] = (
                        stage_kv[0, pl.ds(kr * 8 + x, 32, stride=64), :].astype(BF)
                    )
            return carry

        await_bytes(got_kv.at[h, pl.ds(0, (N - 1) * 64)], kv_recv.at[h])
        lax.fori_loop(0, 4, one, 0)
        await_bytes(pre_k.at[h, pl.ds(0, 3)], pre_recv.at[4 + 2 * h])
        await_bytes(pre_v.at[h, :, pl.ds(0, 3)], pre_recv.at[5 + 2 * h])

    def attend(g, carry):
        h = g >> 2
        columns = pl.ds(pl.multiple_of((g & 3) * HD, HD), HD)
        for y in range(4):
            prefix_keys = pre_k[h, y, :, :, :, columns].reshape(256, HD)
            rows = pl.ds(y * 256, 256)
            keys2[rows, :HD] = prefix_keys
            keys2[rows, HD:] = prefix_keys
            vals2[rows, :HD] = pre_v[h, y, :, :, :, columns].reshape(256, HD)
        keys2[PRE:, :HD] = near[0, g]
        keys2[PRE:, HD:] = near[0, g]
        vals2[PRE:, :HD] = near[1, g]
        await_bytes(got_q.at[g, pl.ds(0, (N - 1) * 16)], q_recv.at[g])
        stage_q[...] = got_q[g].astype(F32)
        for j in range(PER):
            for r in range(2):
                scaled = stage_q[pl.ds(r * PER + j, N, stride=16), :] * SCALE
                high = scaled.astype(BF)
                rows = pl.ds(j * ROWS + r * N, N)
                lhs[rows, :HD] = high
                lhs[rows, HD:] = (scaled - high.astype(F32)).astype(BF)

        def score_step(tile, into, peak, c, top):
            part = lax.dot_general(
                lhs[pl.ds(tile * TILE, TILE), :], keys2[c * WIDE:(c + 1) * WIDE, :],
                (((1,), (1,)), ((), ())), preferred_element_type=F32,
            )
            if c * WIDE >= PRE:
                allowed = mask[:, c * WIDE - PRE:(c + 1) * WIDE - PRE]
                part = part + jnp.concatenate([allowed] * (TILE // ROWS), axis=0)
            into[:, c * WIDE:(c + 1) * WIDE] = part
            for t in range(WIDE // HD):
                piece = part[:, t * HD:(t + 1) * HD]
                top = piece if top is None else jnp.maximum(top, piece)
            if c == KEYS // WIDE - 1:
                peak[...] = jnp.broadcast_to(jnp.max(top, axis=1, keepdims=True), (TILE, HD))
            return top

        def value_step(held, top, c, total):
            shifted = held[:, c * WIDE:(c + 1) * WIDE] - jnp.concatenate([top] * (WIDE // HD), axis=1)
            more = jnp.dot(
                jnp.exp2(shifted).astype(BF), vals2[c * WIDE:(c + 1) * WIDE, :],
                preferred_element_type=F32,
            )
            return more if total is None else total + more

        slots = ((scores_a, peak_a), (scores_b, peak_b))
        for tile in range(TILES + 1):
            into, peak = slots[tile % 2]
            held, held_peak = slots[(tile + 1) % 2]
            top = total = None
            before = held_peak[...] if tile > 0 else None
            for c in range(KEYS // WIDE):
                if tile < TILES:
                    top = score_step(tile, into, peak, c, top)
                if tile > 0:
                    total = value_step(held, before, c, total)
            if tile > 0:
                result = (total[:, :HD] / total[:, HD:]).astype(BF)
                for t in range(TILE // ROWS):
                    j = (tile - 1) * (TILE // ROWS) + t
                    heads_out[:, j * HD:(j + 1) * HD] = result[t * ROWS:(t + 1) * ROWS]
        out_ref[:, pl.ds(pl.multiple_of(g * 1024, 1024), 1024)] = jnp.dot(
            back[...], heads_out[...], preferred_element_type=F32
        ).astype(BF)
        return carry

    unpack_kv(0)
    lax.fori_loop(LATE, GROUPS, spread_q, 0)

    def attend_next(g, carry):
        @pl.when(g == HALF)
        def second_half():
            unpack_kv(1)

        return attend(g, carry)

    lax.fori_loop(0, GROUPS, attend_next, 0)

    def sent_q(g, carry):
        await_bytes(send_q.at[g, pl.ds(0, (N - 1) * 16)], q_send.at[g])
        return carry

    lax.fori_loop(0, GROUPS, sent_q, 0)
    for i, ref in enumerate((pre_k, pre_v)):
        await_bytes(ref.at[:, 0, 0, 0], pre_send.at[i])
    await_bytes(pre_k.at[:, 0, pl.ds(0, 3)], pre_send.at[2])
    await_bytes(pre_v.at[:, pl.ds(0, 3), 0], pre_send.at[3])
    for h in range(2):
        await_bytes(got_kv.at[h, pl.ds(0, (N - 1) * 64)], kv_send.at[h])
        await_bytes(pre_k.at[h, pl.ds(0, 3)], pre_send.at[4 + 2 * h])
        await_bytes(pre_v.at[h, :, pl.ds(0, 3)], pre_send.at[5 + 2 * h])


def per_device(resp_q, resp_k, resp_v, prefix_k, prefix_v, destination, resp_len):
    dest = destination.reshape(N, ROWS)
    vmem = pl.BlockSpec(memory_space=pltpu.VMEM)
    return pl.pallas_call(
        kernel,
        out_shape=jax.ShapeDtypeStruct((ROWS, GROUPS * PER * HD), BF),
        in_specs=[vmem] * 7 + [pl.BlockSpec(memory_space=pltpu.SMEM)],
        out_specs=vmem,
        scratch_shapes=[
            pltpu.VMEM((GROUPS, N * 16, HD), BF),
            pltpu.VMEM((2, 131 * 16, HD), BF),
            pltpu.VMEM((GROUPS, N * 16, HD), BF),
            pltpu.VMEM((2, N * 64, HD), BF),
            pltpu.VMEM((2, 4, 4, 2, 32, HALF * HD), BF),
            pltpu.VMEM((2, 4, 4, 2, 32, HALF * HD), BF),
            pltpu.VMEM((N * 16, HD), F32),
            pltpu.VMEM((2, N * 16, HD), F32),
            pltpu.VMEM((2, GROUPS, NEAR, HD), BF),
            pltpu.VMEM((PER * ROWS, 2 * HD), BF),
            pltpu.VMEM((KEYS, 2 * HD), BF),
            pltpu.VMEM((KEYS, 2 * HD), BF),
            pltpu.VMEM((ROWS, NEAR), F32),
            pltpu.VMEM((ROWS, ROWS), BF),
            pltpu.VMEM((TILE, KEYS), F32),
            pltpu.VMEM((TILE, KEYS), F32),
            pltpu.VMEM((TILE, HD), F32),
            pltpu.VMEM((TILE, HD), F32),
            pltpu.VMEM((ROWS, PER * HD), BF),
            pltpu.SemaphoreType.DMA((GROUPS,)),
            pltpu.SemaphoreType.DMA((GROUPS,)),
            pltpu.SemaphoreType.DMA((2,)),
            pltpu.SemaphoreType.DMA((2,)),
            pltpu.SemaphoreType.DMA((8,)),
            pltpu.SemaphoreType.DMA((8,)),
        ],
        compiler_params=pltpu.CompilerParams(
            collective_id=0, has_side_effects=True, vmem_limit_bytes=60 * 1024 * 1024
        ),
    )(resp_q, resp_k, resp_v, prefix_k, prefix_v, dest, dest.T, resp_len)


def solution(mesh):
    both = P(("prompt", "seq"), None)
    return jax.shard_map(
        per_device,
        mesh=mesh,
        in_specs=(both, both, both, both, both, P(), P("prompt", None)),
        out_specs=both,
        check_vma=False,
    )
```

```python
import functools
import math

import jax
import jax.numpy as jnp
from jax import lax
from jax.experimental import pallas as pl
from jax.experimental.pallas import tpu as pltpu
from jax.sharding import PartitionSpec as P

MESH = pl.DeviceIdType.MESH
N = 128
NS = 32
ROWS = 256
GROUPS = 8
PER = 8
HD = 128
NEAR = 1024
PRE = 1024
KEYS = PRE + NEAR
WIDE = 256
TILE = 512
TILES = PER * ROWS // TILE
SCALE = math.log2(math.e) / math.sqrt(HD)
HALF = 4
LATE = 8
BF = jnp.bfloat16
F32 = jnp.float32


def device_of(index):
    return (index >> 5, index & (NS - 1))


def remote(src, dst, send, recv, device):
    return pltpu.make_async_remote_copy(
        src_ref=src, dst_ref=dst, send_sem=send, recv_sem=recv, device_id=device, device_id_type=MESH
    )


def await_bytes(ref, sem):
    pltpu.make_async_copy(ref, ref, sem).wait()


def iota(shape, dim):
    return lax.broadcasted_iota(jnp.int32, shape, dim).astype(F32)


def kernel(
    q_hbm, k_ref, v_ref, pk_ref, pv_ref, dest_ref, dest_t_ref, len_ref, out_hbm,
    q_ref, out_ref,
    send_q, send_kv, got_q, got_kv, pre_k, pre_v, stage_q, stage_kv, near,
    lhs, keys2, vals2, mask, back, scores_a, scores_b, peak_a, peak_b, heads_out,
    q_send, q_recv, kv_send, kv_recv, pre_send, pre_recv, in_sem, out_sem,
):
    load_q = pltpu.make_async_copy(q_hbm, q_ref, in_sem)
    load_q.start()
    mp = lax.axis_index("prompt")
    ms = lax.axis_index("seq")
    me = mp * NS + ms
    my, mx, mz = ms // 8, lax.rem(ms // 2, 4), lax.rem(ms, 2)

    barrier = pltpu.get_barrier_semaphore()

    def greet(i, carry):
        pl.semaphore_signal(
            barrier, inc=1, device_id=device_of((me + i) & (N - 1)), device_id_type=MESH
        )
        return carry

    lax.fori_loop(1, N, greet, 0)

    dest_t = dest_t_ref[...].astype(F32)
    own_row = dest_ref[pl.ds(me, 1), :].astype(F32)
    me_f = me.astype(F32)
    own_col = jnp.sum(jnp.where(iota((ROWS, N), 1) == me_f, dest_t, 0.0), axis=1, keepdims=True)
    slot = jnp.sum((own_col < own_row).astype(F32), axis=0, keepdims=True)
    packer = (iota((ROWS, ROWS), 0) == slot).astype(BF)

    for i, ref in enumerate((k_ref, v_ref)):
        packed = jnp.dot(packer, ref[...], preferred_element_type=F32)
        for g in range(GROUPS):
            stage_kv[g // HALF, pl.ds(i * HALF + g % HALF, ROWS, stride=8), :] = packed[
                :, g * HD:(g + 1) * HD
            ]
    for h in range(2):
        send_kv[h, pl.ds(0, 48), :] = jnp.zeros((48, HD), BF)
        send_kv[h, pl.ds(48, 2048), :] = stage_kv[h].astype(BF)
        got_kv[h, pl.ds(pl.multiple_of(me * 64, 64), 64), :] = send_kv[
            h, pl.ds(pl.multiple_of(me * 16, 16), 64), :
        ]
        pre_k[h, my, mx, mz] = pk_ref[:, h * HALF * HD:(h + 1) * HALF * HD]
        pre_v[h, my, mx, mz] = pv_ref[:, h * HALF * HD:(h + 1) * HALF * HD]

    pl.semaphore_wait(barrier, N - 1)

    def along_x(k):
        return (mp, my * 8 + lax.rem(mx + k, 4) * 2 + mz)

    def along_y(k):
        return (mp, lax.rem(my + k, 4) * 8 + mx * 2 + mz)

    across = (mp, ms + 1 - 2 * mz)
    for i, ref in enumerate((pre_k, pre_v)):
        own = ref.at[:, my, mx, mz]
        remote(own, own, pre_send.at[i], pre_recv.at[i], across).start()

    def spread_kv(h, i):
        to = (me + i) & (N - 1)
        remote(
            send_kv.at[h, pl.ds(pl.multiple_of(to * 16, 16), 64)],
            got_kv.at[h, pl.ds(pl.multiple_of(me * 64, 64), 64)],
            kv_send.at[h], kv_recv.at[h], device_of(to),
        ).start()

    def spread_kv_part(h, first, last):
        def one(i, carry):
            spread_kv(h, i)
            return carry

        lax.fori_loop(first, last, one, 0, unroll=4)

    def spread_prefix(h, first):
        def one(n, carry):
            k, b = (n >> 2) + 1, n & 3
            piece = pre_k.at[h, my, b]
            remote(piece, piece, pre_send.at[4 + 2 * h], pre_recv.at[4 + 2 * h], along_y(k)).start()
            spread_kv(h, first + 2 * n)
            piece = pre_v.at[h, b, mx]
            remote(piece, piece, pre_send.at[5 + 2 * h], pre_recv.at[5 + 2 * h], along_x(k)).start()
            spread_kv(h, first + 2 * n + 1)
            return carry

        lax.fori_loop(0, 12, one, 0)

    spread_kv_part(0, 1, 41)
    for i, ref in enumerate((pre_k, pre_v)):
        await_bytes(ref.at[:, 0, 0, 0], pre_recv.at[i])
    for k in (1, 3, 2):
        piece = pre_k.at[:, my, mx]
        remote(piece, piece, pre_send.at[2], pre_recv.at[2], along_x(k)).start()
        piece = pre_v.at[:, my, mx]
        remote(piece, piece, pre_send.at[3], pre_recv.at[3], along_y(k)).start()
    spread_kv_part(0, 41, 81)

    def pack(g, carry):
        packed = jnp.dot(
            packer, q_ref[:, pl.ds(pl.multiple_of(g * 1024, 1024), 1024)],
            preferred_element_type=F32,
        )
        for j in range(PER):
            stage_q[pl.ds(j, ROWS, stride=PER), :] = packed[:, j * HD:(j + 1) * HD]
        send_q[g] = stage_q[...].astype(BF)
        own = pl.ds(pl.multiple_of(me * 16, 16), 16)
        got_q[g, own, :] = send_q[g, own, :]
        return carry

    load_q.wait()
    lax.fori_loop(0, GROUPS, pack, 0)

    dest = dest_ref[...].astype(F32)
    base = me_f * ROWS
    here = (dest >= base) & (dest < base + ROWS)
    pos_q = jnp.concatenate(
        [
            jnp.min(jnp.where(here, dest, 1e9), axis=1, keepdims=True),
            jnp.max(jnp.where(here, dest, -1.0), axis=1, keepdims=True),
        ],
        axis=0,
    )
    prompt_base = (mp * (NS * ROWS)).astype(F32)
    start = jnp.zeros((ROWS, 1), F32) + prompt_base
    finish = prompt_base
    for c in range(16):
        length = len_ref[0, c].astype(F32)
        finish = finish + length
        start = start + jnp.where(pos_q >= finish, length, 0.0)
    pos_rows = []
    for k in range(4):
        low = base + (k - 3) * ROWS
        inside = (dest_t >= low) & (dest_t < low + ROWS)
        first = jnp.min(jnp.where(inside, dest_t, 1e9), axis=0, keepdims=True)
        last = jnp.max(jnp.where(inside, dest_t, -1.0), axis=0, keepdims=True)
        pos_rows.append((first, last))
    for k in range(4):
        for r in range(2):
            pos_k = pos_rows[k][r]
            mask[:, (2 * k + r) * N:(2 * k + r + 1) * N] = jnp.where(
                (pos_k >= start) & (pos_k <= pos_q), 0.0, -1e30
            )
    for r in range(2):
        back[:, r * N:(r + 1) * N] = (iota((ROWS, N), 0) == pos_rows[3][r] - base).astype(BF)
    vals2[:, HD:] = jnp.ones((KEYS, HD), BF)

    def spread_q(g, carry):
        def one(i, inner):
            to = (me + i) & (N - 1)
            remote(
                send_q.at[g, pl.ds(pl.multiple_of(to * 16, 16), 16)],
                got_q.at[g, pl.ds(pl.multiple_of(me * 16, 16), 16)],
                q_send.at[g], q_recv.at[g], device_of(to),
            ).start()
            return inner

        return lax.fori_loop(1, N, one, carry, unroll=8)

    await_bytes(pre_k.at[:, 0, pl.ds(0, 3)], pre_recv.at[2])
    await_bytes(pre_v.at[:, pl.ds(0, 3), 0], pre_recv.at[3])
    spread_prefix(0, 81)
    spread_kv_part(0, 105, N)
    lax.fori_loop(0, HALF, spread_q, 0)
    spread_kv_part(1, 1, 41)
    spread_prefix(1, 41)
    spread_kv_part(1, 65, N)
    lax.fori_loop(HALF, LATE, spread_q, 0)

    def unpack_kv(h):
        def one(p, carry):
            stage_kv[0] = got_kv[h, pl.ds(pl.multiple_of(p * 2048, 2048), 2048), :].astype(F32)
            for x in range(8):
                for kr in range(8):
                    near[x // HALF, h * HALF + x % HALF, pl.ds(pl.multiple_of(kr * N + p * 32, 32), 32), :] = (
                        stage_kv[0, pl.ds(kr * 8 + x, 32, stride=64), :].astype(BF)
                    )
            return carry

        await_bytes(got_kv.at[h, pl.ds(0, (N - 1) * 64)], kv_recv.at[h])
        lax.fori_loop(0, 4, one, 0)
        await_bytes(pre_k.at[h, pl.ds(0, 3)], pre_recv.at[4 + 2 * h])
        await_bytes(pre_v.at[h, :, pl.ds(0, 3)], pre_recv.at[5 + 2 * h])

    def store_out(g):
        columns = pl.ds(pl.multiple_of(g * 1024, 1024), 1024)
        return pltpu.make_async_copy(out_ref.at[:, columns], out_hbm.at[:, columns], out_sem.at[g])

    def attend(g, carry):
        h = g >> 2
        columns = pl.ds(pl.multiple_of((g & 3) * HD, HD), HD)
        for y in range(4):
            prefix_keys = pre_k[h, y, :, :, :, columns].reshape(256, HD)
            rows = pl.ds(y * 256, 256)
            keys2[rows, :HD] = prefix_keys
            keys2[rows, HD:] = prefix_keys
            vals2[rows, :HD] = pre_v[h, y, :, :, :, columns].reshape(256, HD)
        keys2[PRE:, :HD] = near[0, g]
        keys2[PRE:, HD:] = near[0, g]
        vals2[PRE:, :HD] = near[1, g]
        await_bytes(got_q.at[g, pl.ds(0, (N - 1) * 16)], q_recv.at[g])
        stage_q[...] = got_q[g].astype(F32)
        for j in range(PER):
            for r in range(2):
                scaled = stage_q[pl.ds(r * PER + j, N, stride=16), :] * SCALE
                high = scaled.astype(BF)
                rows = pl.ds(j * ROWS + r * N, N)
                lhs[rows, :HD] = high
                lhs[rows, HD:] = (scaled - high.astype(F32)).astype(BF)

        def score_step(tile, into, peak, c, top):
            part = lax.dot_general(
                lhs[pl.ds(tile * TILE, TILE), :], keys2[c * WIDE:(c + 1) * WIDE, :],
                (((1,), (1,)), ((), ())), preferred_element_type=F32,
            )
            if c * WIDE >= PRE:
                allowed = mask[:, c * WIDE - PRE:(c + 1) * WIDE - PRE]
                part = part + jnp.concatenate([allowed] * (TILE // ROWS), axis=0)
            into[:, c * WIDE:(c + 1) * WIDE] = part
            for t in range(WIDE // HD):
                piece = part[:, t * HD:(t + 1) * HD]
                top = piece if top is None else jnp.maximum(top, piece)
            if c == KEYS // WIDE - 1:
                peak[...] = jnp.broadcast_to(jnp.max(top, axis=1, keepdims=True), (TILE, HD))
            return top

        def value_step(held, top, c, total):
            shifted = held[:, c * WIDE:(c + 1) * WIDE] - jnp.concatenate([top] * (WIDE // HD), axis=1)
            more = jnp.dot(
                jnp.exp2(shifted).astype(BF), vals2[c * WIDE:(c + 1) * WIDE, :],
                preferred_element_type=F32,
            )
            return more if total is None else total + more

        slots = ((scores_a, peak_a), (scores_b, peak_b))
        for tile in range(TILES + 1):
            into, peak = slots[tile % 2]
            held, held_peak = slots[(tile + 1) % 2]
            top = total = None
            before = held_peak[...] if tile > 0 else None
            for c in range(KEYS // WIDE):
                if tile < TILES:
                    top = score_step(tile, into, peak, c, top)
                if tile > 0:
                    total = value_step(held, before, c, total)
            if tile > 0:
                result = (total[:, :HD] / total[:, HD:]).astype(BF)
                for t in range(TILE // ROWS):
                    j = (tile - 1) * (TILE // ROWS) + t
                    heads_out[:, j * HD:(j + 1) * HD] = result[t * ROWS:(t + 1) * ROWS]
        out_ref[:, pl.ds(pl.multiple_of(g * 1024, 1024), 1024)] = jnp.dot(
            back[...], heads_out[...], preferred_element_type=F32
        ).astype(BF)
        store_out(g).start()
        return carry

    unpack_kv(0)
    lax.fori_loop(LATE, GROUPS, spread_q, 0)

    def attend_next(g, carry):
        @pl.when(g == HALF)
        def second_half():
            unpack_kv(1)

        return attend(g, carry)

    lax.fori_loop(0, GROUPS, attend_next, 0)

    def sent_q(g, carry):
        store_out(g).wait()
        await_bytes(send_q.at[g, pl.ds(0, (N - 1) * 16)], q_send.at[g])
        return carry

    lax.fori_loop(0, GROUPS, sent_q, 0)
    for i, ref in enumerate((pre_k, pre_v)):
        await_bytes(ref.at[:, 0, 0, 0], pre_send.at[i])
    await_bytes(pre_k.at[:, 0, pl.ds(0, 3)], pre_send.at[2])
    await_bytes(pre_v.at[:, pl.ds(0, 3), 0], pre_send.at[3])
    for h in range(2):
        await_bytes(got_kv.at[h, pl.ds(0, (N - 1) * 64)], kv_send.at[h])
        await_bytes(pre_k.at[h, pl.ds(0, 3)], pre_send.at[4 + 2 * h])
        await_bytes(pre_v.at[h, :, pl.ds(0, 3)], pre_send.at[5 + 2 * h])


def per_device(resp_q, resp_k, resp_v, prefix_k, prefix_v, destination, resp_len):
    dest = destination.reshape(N, ROWS)
    vmem = pl.BlockSpec(memory_space=pltpu.VMEM)
    anywhere = pl.BlockSpec(memory_space=pl.ANY)
    return pl.pallas_call(
        kernel,
        out_shape=jax.ShapeDtypeStruct((ROWS, GROUPS * PER * HD), BF),
        in_specs=[anywhere] + [vmem] * 6 + [pl.BlockSpec(memory_space=pltpu.SMEM)],
        out_specs=anywhere,
        scratch_shapes=[
            pltpu.VMEM((ROWS, GROUPS * PER * HD), BF),
            pltpu.VMEM((ROWS, GROUPS * PER * HD), BF),
            pltpu.VMEM((GROUPS, N * 16, HD), BF),
            pltpu.VMEM((2, 131 * 16, HD), BF),
            pltpu.VMEM((GROUPS, N * 16, HD), BF),
            pltpu.VMEM((2, N * 64, HD), BF),
            pltpu.VMEM((2, 4, 4, 2, 32, HALF * HD), BF),
            pltpu.VMEM((2, 4, 4, 2, 32, HALF * HD), BF),
            pltpu.VMEM((N * 16, HD), F32),
            pltpu.VMEM((2, N * 16, HD), F32),
            pltpu.VMEM((2, GROUPS, NEAR, HD), BF),
            pltpu.VMEM((PER * ROWS, 2 * HD), BF),
            pltpu.VMEM((KEYS, 2 * HD), BF),
            pltpu.VMEM((KEYS, 2 * HD), BF),
            pltpu.VMEM((ROWS, NEAR), F32),
            pltpu.VMEM((ROWS, ROWS), BF),
            pltpu.VMEM((TILE, KEYS), F32),
            pltpu.VMEM((TILE, KEYS), F32),
            pltpu.VMEM((TILE, HD), F32),
            pltpu.VMEM((TILE, HD), F32),
            pltpu.VMEM((ROWS, PER * HD), BF),
            pltpu.SemaphoreType.DMA((GROUPS,)),
            pltpu.SemaphoreType.DMA((GROUPS,)),
            pltpu.SemaphoreType.DMA((2,)),
            pltpu.SemaphoreType.DMA((2,)),
            pltpu.SemaphoreType.DMA((8,)),
            pltpu.SemaphoreType.DMA((8,)),
            pltpu.SemaphoreType.DMA,
            pltpu.SemaphoreType.DMA((GROUPS,)),
        ],
        compiler_params=pltpu.CompilerParams(
            collective_id=0, has_side_effects=True, vmem_limit_bytes=60 * 1024 * 1024
        ),
    )(resp_q, resp_k, resp_v, prefix_k, prefix_v, dest, dest.T, resp_len)


def solution(mesh):
    both = P(("prompt", "seq"), None)
    return jax.shard_map(
        per_device,
        mesh=mesh,
        in_specs=(both, both, both, both, both, P(), P("prompt", None)),
        out_specs=both,
        check_vma=False,
    )
```

```python
import functools
import math

import jax
import jax.numpy as jnp
from jax import lax
from jax.experimental import pallas as pl
from jax.experimental.pallas import tpu as pltpu
from jax.sharding import PartitionSpec as P

MESH = pl.DeviceIdType.MESH
N = 128
NS = 32
ROWS = 256
GROUPS = 8
PER = 8
HD = 128
NEAR = 1024
PRE = 1024
KEYS = PRE + NEAR
WIDE = 256
TILE = 512
TILES = PER * ROWS // TILE
SCALE = math.log2(math.e) / math.sqrt(HD)
HALF = 4
FIRST = 2
BF = jnp.bfloat16
F32 = jnp.float32


def device_of(index):
    return (index >> 5, index & (NS - 1))


def remote(src, dst, send, recv, device):
    return pltpu.make_async_remote_copy(
        src_ref=src, dst_ref=dst, send_sem=send, recv_sem=recv, device_id=device, device_id_type=MESH
    )


def await_bytes(ref, sem):
    pltpu.make_async_copy(ref, ref, sem).wait()


def iota(shape, dim):
    return lax.broadcasted_iota(jnp.int32, shape, dim).astype(F32)


def kernel(
    q_hbm, k_ref, v_ref, pk_ref, pv_ref, dest_ref, dest_t_ref, len_ref, out_hbm,
    q_ref, out_ref,
    send_q, send_kv, got_q, got_kv, pre_k, pre_v, stage_q, stage_kv, near,
    lhs, keys2, vals2, mask, back, scores_a, scores_b, peak_a, peak_b, heads_out,
    q_send, q_recv, kv_send, kv_recv, pre_send, pre_recv, in_sem, out_sem,
):
    load_q = pltpu.make_async_copy(q_hbm, q_ref, in_sem)
    load_q.start()
    mp = lax.axis_index("prompt")
    ms = lax.axis_index("seq")
    me = mp * NS + ms
    my, mx, mz = ms // 8, lax.rem(ms // 2, 4), lax.rem(ms, 2)

    barrier = pltpu.get_barrier_semaphore()

    def greet(i, carry):
        pl.semaphore_signal(
            barrier, inc=1, device_id=device_of((me + i) & (N - 1)), device_id_type=MESH
        )
        return carry

    lax.fori_loop(1, N, greet, 0)

    dest_t = dest_t_ref[...].astype(F32)
    own_row = dest_ref[pl.ds(me, 1), :].astype(F32)
    me_f = me.astype(F32)
    own_col = jnp.sum(jnp.where(iota((ROWS, N), 1) == me_f, dest_t, 0.0), axis=1, keepdims=True)
    slot = jnp.sum((own_col < own_row).astype(F32), axis=0, keepdims=True)
    packer = (iota((ROWS, ROWS), 0) == slot).astype(BF)

    for i, ref in enumerate((k_ref, v_ref)):
        packed = jnp.dot(packer, ref[...], preferred_element_type=F32)
        for g in range(GROUPS):
            stage_kv[g // HALF, pl.ds(i * HALF + g % HALF, ROWS, stride=8), :] = packed[
                :, g * HD:(g + 1) * HD
            ]
    for h in range(2):
        send_kv[h, pl.ds(0, 48), :] = jnp.zeros((48, HD), BF)
        send_kv[h, pl.ds(48, 2048), :] = stage_kv[h].astype(BF)
        got_kv[h, pl.ds(pl.multiple_of(me * 64, 64), 64), :] = send_kv[
            h, pl.ds(pl.multiple_of(me * 16, 16), 64), :
        ]
        pre_k[h, my, mx, mz] = pk_ref[:, h * HALF * HD:(h + 1) * HALF * HD]
        pre_v[h, my, mx, mz] = pv_ref[:, h * HALF * HD:(h + 1) * HALF * HD]

    pl.semaphore_wait(barrier, N - 1)

    def along_x(k):
        return (mp, my * 8 + lax.rem(mx + k, 4) * 2 + mz)

    def along_y(k):
        return (mp, lax.rem(my + k, 4) * 8 + mx * 2 + mz)

    across = (mp, ms + 1 - 2 * mz)
    for i, ref in enumerate((pre_k, pre_v)):
        own = ref.at[:, my, mx, mz]
        remote(own, own, pre_send.at[i], pre_recv.at[i], across).start()

    def spread_kv(h, i):
        to = (me + i) & (N - 1)
        remote(
            send_kv.at[h, pl.ds(pl.multiple_of(to * 16, 16), 64)],
            got_kv.at[h, pl.ds(pl.multiple_of(me * 64, 64), 64)],
            kv_send.at[h], kv_recv.at[h], device_of(to),
        ).start()

    def spread_kv_part(h, first, last):
        def one(i, carry):
            spread_kv(h, i)
            return carry

        lax.fori_loop(first, last, one, 0, unroll=4)

    def spread_prefix(h, first):
        def one(n, carry):
            k, b = (n >> 2) + 1, n & 3
            piece = pre_k.at[h, my, b]
            remote(piece, piece, pre_send.at[4 + 2 * h], pre_recv.at[4 + 2 * h], along_y(k)).start()
            spread_kv(h, first + 2 * n)
            piece = pre_v.at[h, b, mx]
            remote(piece, piece, pre_send.at[5 + 2 * h], pre_recv.at[5 + 2 * h], along_x(k)).start()
            spread_kv(h, first + 2 * n + 1)
            return carry

        lax.fori_loop(0, 12, one, 0)

    spread_kv_part(0, 1, 41)
    for i, ref in enumerate((pre_k, pre_v)):
        await_bytes(ref.at[:, 0, 0, 0], pre_recv.at[i])
    for k in (1, 3, 2):
        piece = pre_k.at[:, my, mx]
        remote(piece, piece, pre_send.at[2], pre_recv.at[2], along_x(k)).start()
        piece = pre_v.at[:, my, mx]
        remote(piece, piece, pre_send.at[3], pre_recv.at[3], along_y(k)).start()
    spread_kv_part(0, 41, 81)

    def pack(g, carry):
        packed = jnp.dot(
            packer, q_ref[:, pl.ds(pl.multiple_of(g * 1024, 1024), 1024)],
            preferred_element_type=F32,
        )
        for j in range(PER):
            stage_q[pl.ds(j, ROWS, stride=PER), :] = packed[:, j * HD:(j + 1) * HD]
        send_q[g] = stage_q[...].astype(BF)
        own = pl.ds(pl.multiple_of(me * 16, 16), 16)
        got_q[g, own, :] = send_q[g, own, :]
        return carry

    load_q.wait()
    lax.fori_loop(0, GROUPS, pack, 0)

    dest = dest_ref[...].astype(F32)
    base = me_f * ROWS
    here = (dest >= base) & (dest < base + ROWS)
    pos_q = jnp.concatenate(
        [
            jnp.min(jnp.where(here, dest, 1e9), axis=1, keepdims=True),
            jnp.max(jnp.where(here, dest, -1.0), axis=1, keepdims=True),
        ],
        axis=0,
    )
    prompt_base = (mp * (NS * ROWS)).astype(F32)
    start = jnp.zeros((ROWS, 1), F32) + prompt_base
    finish = prompt_base
    for c in range(16):
        length = len_ref[0, c].astype(F32)
        finish = finish + length
        start = start + jnp.where(pos_q >= finish, length, 0.0)
    pos_rows = []
    for k in range(4):
        low = base + (k - 3) * ROWS
        inside = (dest_t >= low) & (dest_t < low + ROWS)
        first = jnp.min(jnp.where(inside, dest_t, 1e9), axis=0, keepdims=True)
        last = jnp.max(jnp.where(inside, dest_t, -1.0), axis=0, keepdims=True)
        pos_rows.append((first, last))
    for k in range(4):
        for r in range(2):
            pos_k = pos_rows[k][r]
            mask[:, (2 * k + r) * N:(2 * k + r + 1) * N] = jnp.where(
                (pos_k >= start) & (pos_k <= pos_q), 0.0, -1e30
            )
    for r in range(2):
        back[:, r * N:(r + 1) * N] = (iota((ROWS, N), 0) == pos_rows[3][r] - base).astype(BF)
    vals2[:, HD:] = jnp.ones((KEYS, HD), BF)

    def spread_q(g, carry):
        def one(i, inner):
            to = (me + i) & (N - 1)
            remote(
                send_q.at[g, pl.ds(pl.multiple_of(to * 16, 16), 16)],
                got_q.at[g, pl.ds(pl.multiple_of(me * 16, 16), 16)],
                q_send.at[g], q_recv.at[g], device_of(to),
            ).start()
            return inner

        return lax.fori_loop(1, N, one, carry, unroll=8)

    await_bytes(pre_k.at[:, 0, pl.ds(0, 3)], pre_recv.at[2])
    await_bytes(pre_v.at[:, pl.ds(0, 3), 0], pre_recv.at[3])
    spread_prefix(0, 81)
    spread_kv_part(0, 105, N)
    lax.fori_loop(0, FIRST, spread_q, 0)
    spread_kv_part(1, 1, 41)
    spread_prefix(1, 41)
    spread_kv_part(1, 65, N)
    lax.fori_loop(FIRST, GROUPS, spread_q, 0)

    def unpack_kv(h):
        def one(p, carry):
            stage_kv[0] = got_kv[h, pl.ds(pl.multiple_of(p * 2048, 2048), 2048), :].astype(F32)
            for x in range(8):
                for kr in range(8):
                    near[x // HALF, h * HALF + x % HALF, pl.ds(pl.multiple_of(kr * N + p * 32, 32), 32), :] = (
                        stage_kv[0, pl.ds(kr * 8 + x, 32, stride=64), :].astype(BF)
                    )
            return carry

        await_bytes(got_kv.at[h, pl.ds(0, (N - 1) * 64)], kv_recv.at[h])
        lax.fori_loop(0, 4, one, 0)
        await_bytes(pre_k.at[h, pl.ds(0, 3)], pre_recv.at[4 + 2 * h])
        await_bytes(pre_v.at[h, :, pl.ds(0, 3)], pre_recv.at[5 + 2 * h])

    def store_out(g):
        columns = pl.ds(pl.multiple_of(g * 1024, 1024), 1024)
        return pltpu.make_async_copy(out_ref.at[:, columns], out_hbm.at[:, columns], out_sem.at[g])

    def attend(g, carry):
        h = g >> 2
        columns = pl.ds(pl.multiple_of((g & 3) * HD, HD), HD)
        for y in range(4):
            prefix_keys = pre_k[h, y, :, :, :, columns].reshape(256, HD)
            rows = pl.ds(y * 256, 256)
            keys2[rows, :HD] = prefix_keys
            keys2[rows, HD:] = prefix_keys
            vals2[rows, :HD] = pre_v[h, y, :, :, :, columns].reshape(256, HD)
        keys2[PRE:, :HD] = near[0, g]
        keys2[PRE:, HD:] = near[0, g]
        vals2[PRE:, :HD] = near[1, g]
        await_bytes(got_q.at[g, pl.ds(0, (N - 1) * 16)], q_recv.at[g])
        stage_q[...] = got_q[g].astype(F32)
        for j in range(PER):
            for r in range(2):
                scaled = stage_q[pl.ds(r * PER + j, N, stride=16), :] * SCALE
                high = scaled.astype(BF)
                rows = pl.ds(j * ROWS + r * N, N)
                lhs[rows, :HD] = high
                lhs[rows, HD:] = (scaled - high.astype(F32)).astype(BF)

        def score_step(tile, into, peak, c, top):
            part = lax.dot_general(
                lhs[pl.ds(tile * TILE, TILE), :], keys2[c * WIDE:(c + 1) * WIDE, :],
                (((1,), (1,)), ((), ())), preferred_element_type=F32,
            )
            if c * WIDE >= PRE:
                allowed = mask[:, c * WIDE - PRE:(c + 1) * WIDE - PRE]
                part = part + jnp.concatenate([allowed] * (TILE // ROWS), axis=0)
            into[:, c * WIDE:(c + 1) * WIDE] = part
            for t in range(WIDE // HD):
                piece = part[:, t * HD:(t + 1) * HD]
                top = piece if top is None else jnp.maximum(top, piece)
            if c == KEYS // WIDE - 1:
                peak[...] = jnp.broadcast_to(jnp.max(top, axis=1, keepdims=True), (TILE, HD))
            return top

        def value_step(held, top, c, total):
            shifted = held[:, c * WIDE:(c + 1) * WIDE] - jnp.concatenate([top] * (WIDE // HD), axis=1)
            more = jnp.dot(
                jnp.exp2(shifted).astype(BF), vals2[c * WIDE:(c + 1) * WIDE, :],
                preferred_element_type=F32,
            )
            return more if total is None else total + more

        slots = ((scores_a, peak_a), (scores_b, peak_b))
        for tile in range(TILES + 1):
            into, peak = slots[tile % 2]
            held, held_peak = slots[(tile + 1) % 2]
            top = total = None
            before = held_peak[...] if tile > 0 else None
            for c in range(KEYS // WIDE):
                if tile < TILES:
                    top = score_step(tile, into, peak, c, top)
                if tile > 0:
                    total = value_step(held, before, c, total)
            if tile > 0:
                result = (total[:, :HD] / total[:, HD:]).astype(BF)
                for t in range(TILE // ROWS):
                    j = (tile - 1) * (TILE // ROWS) + t
                    heads_out[:, j * HD:(j + 1) * HD] = result[t * ROWS:(t + 1) * ROWS]
        out_ref[:, pl.ds(pl.multiple_of(g * 1024, 1024), 1024)] = jnp.dot(
            back[...], heads_out[...], preferred_element_type=F32
        ).astype(BF)
        store_out(g).start()
        return carry

    unpack_kv(0)

    def attend_next(g, carry):
        @pl.when(g == HALF)
        def second_half():
            unpack_kv(1)

        return attend(g, carry)

    lax.fori_loop(0, GROUPS, attend_next, 0)

    def sent_q(g, carry):
        store_out(g).wait()
        await_bytes(send_q.at[g, pl.ds(0, (N - 1) * 16)], q_send.at[g])
        return carry

    lax.fori_loop(0, GROUPS, sent_q, 0)
    for i, ref in enumerate((pre_k, pre_v)):
        await_bytes(ref.at[:, 0, 0, 0], pre_send.at[i])
    await_bytes(pre_k.at[:, 0, pl.ds(0, 3)], pre_send.at[2])
    await_bytes(pre_v.at[:, pl.ds(0, 3), 0], pre_send.at[3])
    for h in range(2):
        await_bytes(got_kv.at[h, pl.ds(0, (N - 1) * 64)], kv_send.at[h])
        await_bytes(pre_k.at[h, pl.ds(0, 3)], pre_send.at[4 + 2 * h])
        await_bytes(pre_v.at[h, :, pl.ds(0, 3)], pre_send.at[5 + 2 * h])


def per_device(resp_q, resp_k, resp_v, prefix_k, prefix_v, destination, resp_len):
    dest = destination.reshape(N, ROWS)
    vmem = pl.BlockSpec(memory_space=pltpu.VMEM)
    anywhere = pl.BlockSpec(memory_space=pl.ANY)
    return pl.pallas_call(
        kernel,
        out_shape=jax.ShapeDtypeStruct((ROWS, GROUPS * PER * HD), BF),
        in_specs=[anywhere] + [vmem] * 6 + [pl.BlockSpec(memory_space=pltpu.SMEM)],
        out_specs=anywhere,
        scratch_shapes=[
            pltpu.VMEM((ROWS, GROUPS * PER * HD), BF),
            pltpu.VMEM((ROWS, GROUPS * PER * HD), BF),
            pltpu.VMEM((GROUPS, N * 16, HD), BF),
            pltpu.VMEM((2, 131 * 16, HD), BF),
            pltpu.VMEM((GROUPS, N * 16, HD), BF),
            pltpu.VMEM((2, N * 64, HD), BF),
            pltpu.VMEM((2, 4, 4, 2, 32, HALF * HD), BF),
            pltpu.VMEM((2, 4, 4, 2, 32, HALF * HD), BF),
            pltpu.VMEM((N * 16, HD), F32),
            pltpu.VMEM((2, N * 16, HD), F32),
            pltpu.VMEM((2, GROUPS, NEAR, HD), BF),
            pltpu.VMEM((PER * ROWS, 2 * HD), BF),
            pltpu.VMEM((KEYS, 2 * HD), BF),
            pltpu.VMEM((KEYS, 2 * HD), BF),
            pltpu.VMEM((ROWS, NEAR), F32),
            pltpu.VMEM((ROWS, ROWS), BF),
            pltpu.VMEM((TILE, KEYS), F32),
            pltpu.VMEM((TILE, KEYS), F32),
            pltpu.VMEM((TILE, HD), F32),
            pltpu.VMEM((TILE, HD), F32),
            pltpu.VMEM((ROWS, PER * HD), BF),
            pltpu.SemaphoreType.DMA((GROUPS,)),
            pltpu.SemaphoreType.DMA((GROUPS,)),
            pltpu.SemaphoreType.DMA((2,)),
            pltpu.SemaphoreType.DMA((2,)),
            pltpu.SemaphoreType.DMA((8,)),
            pltpu.SemaphoreType.DMA((8,)),
            pltpu.SemaphoreType.DMA,
            pltpu.SemaphoreType.DMA((GROUPS,)),
        ],
        compiler_params=pltpu.CompilerParams(
            collective_id=0, has_side_effects=True, vmem_limit_bytes=60 * 1024 * 1024
        ),
    )(resp_q, resp_k, resp_v, prefix_k, prefix_v, dest, dest.T, resp_len)


def solution(mesh):
    both = P(("prompt", "seq"), None)
    return jax.shard_map(
        per_device,
        mesh=mesh,
        in_specs=(both, both, both, both, both, P(), P("prompt", None)),
        out_specs=both,
        check_vma=False,
    )
```
